32 devices in a mesh: branch: 2 (over y), axial: 8 (over z, x), sub: 2 (over core).
Axes of the slice: x: 2, y: 2, z: 4, core: 2. Of those that a mesh axis runs over, the one named last changes fastest.
Arguments:
- lineup_embedding: bfloat16 [32, 32, 256], P(('branch', 'sub'), 'axial'), may hold values from -6 to 6
- pair_features: bfloat16 [32, 32, 128], P('axial', ('branch', 'sub')), may hold values from -6 to 6
- lineup_entry_keep: int32 [32], replicated, may hold values 0 or 1
- residue_mask: int32 [32], replicated, may hold values 0 or 1
- residue_chain_index: int32 [32], replicated, may hold values from 0 to 3, never falling along the last dimension, each value on 1 to 16 neighbouring positions
- intra_chain_bias: float32 [8], replicated, may hold values from -4 to 4
- pair_bias_weight: bfloat16 [128, 8], replicated, may hold values from -0.5 to 0.5
- attention_weight: bfloat16 [256, 1024], replicated, may hold values from -6 to 6
- final_linear_matrix: bfloat16 [256, 256], replicated, may hold values from -0.375 to 0.375
- tensor_side_matrix: bfloat16 [256, 64], replicated, may hold values from -0.375 to 0.375
- outer_project_weight: bfloat16 [1024, 128], replicated, may hold values from -1 to 1
Outputs:
- alignment_output: bfloat16 [32, 32, 256], P(('branch', 'sub'), 'axial')
- pair_delta_update: bfloat16 [32, 32, 128], P('axial', ('branch', 'sub'))
The draws below stay inside these ranges and needn't reach their ends.
Inputs may be any that keep to these rules, and one draw needn't show every extreme that they name: `residue_chain_index`: chain numbers never fall along the residues; at most 4 chains, one of 16 residues.
All inputs are finite; a program needn't handle non-finite values.
Results may differ from the reference program's by a relative error of at most 0.0094.
Values may be sent and summed in bfloat16 or wider, within the bound.
A program may use at most 64 MiB of HBM per device.

```python
import math
import jax
import jax.numpy as jnp
import numpy as np
from jax import lax

LINEUP_WIDTH = 256
CZ = 128
HEAD_COUNT = 8
HEAD_SPAN = 32
SIDE_WIDTH = 32
AMINO_COUNT = 32
LINEUP_DEPTH = 32
N_BRANCH = 2
N_SUB = 2


def draw_attention_weight(key, part):
    key = jax.random.fold_in(key, 11)
    single_head_span = HEAD_COUNT * HEAD_SPAN
    leading_random_seed = jax.random.fold_in(key, 0)
    gaussian_draw = jax.random.truncated_normal(leading_random_seed, -6.0, 6.0, (LINEUP_WIDTH, 4 * single_head_span), jnp.float32)
    return (gaussian_draw * LINEUP_WIDTH ** (-0.5)).astype(jnp.bfloat16)


def set_ends(array, key, low, top_value):
    longest = array.shape.index(max(array.shape))
    spots = []
    for shift in (0, 1):
        where = [jax.random.randint(jax.random.fold_in(key, axis), (), 0, length) for axis, length in enumerate(array.shape)]
        where[longest] = (where[longest] + shift) % array.shape[longest]
        spots.append(tuple(where))
    return array.at[spots[0]].set(low).at[spots[1]].set(top_value)


def shard_levels(rng, extent, pieces, low, high):
    def one(axis_at, parts):
        heights = jax.random.uniform(jax.random.fold_in(jax.random.fold_in(rng, 6), axis_at), (parts,), jnp.float32, low / len(pieces), high / len(pieces))
        return jnp.repeat(jnp.exp(heights), extent[axis_at] // parts).reshape((-1,) + (1,) * (len(extent) - axis_at - 1))

    loudness = one(*pieces[0])
    for cut in pieces[1:]:
        loudness = loudness * one(*cut)
    return loudness


def split_up(number_of, total, limit, slope):
    loads = [(1 << 20) // math.isqrt(rank ** slope) + 1 for rank in range(2, number_of + 1)]
    rest, counts = total - limit - (number_of - 1), [1] * (number_of - 1)
    while rest > 0:
        candidates = [i for i in range(number_of - 1) if counts[i] < limit]
        whole, left = sum([loads[i] for i in candidates]), rest
        for i in candidates:
            more = min(limit - counts[i], max(1, left * loads[i] // whole), rest)
            counts[i] = counts[i] + more
            rest = rest - more
    return np.array([limit] + counts)


def ragged_sizes(rng, amount, total, most, skew):
    if amount == 2:
        one = jax.random.randint(rng, (), max(1, total - most), min(most, total - 1) + 1)
        return jnp.stack([one, total - one])
    tallies = jnp.asarray(split_up(amount, total, most, skew), jnp.int32)
    twos = (amount - 1) // 2
    giver, receiver = tallies[1:1 + 2 * twos:2], tallies[2:2 + 2 * twos:2]
    slack = jnp.minimum(giver - 1, most - receiver)
    passed = jax.random.randint(jax.random.fold_in(rng, 1), (twos,), 0, 1 << 20) % (slack + 1)
    tallies = tallies.at[1:1 + 2 * twos:2].set(giver - passed).at[2:2 + 2 * twos:2].set(receiver + passed)
    return tallies[jax.random.permutation(jax.random.fold_in(rng, 2), amount)]


def bell_draw(own_key, shape, scale, bound, cuts=(), kind=jnp.bfloat16):
    gain = shard_levels(own_key, shape, cuts, -0.22, 0.18) if cuts else 1.0
    result = jax.random.normal(own_key, shape, jnp.float32) * scale * gain
    return jnp.minimum(jnp.maximum(result, -bound), bound).astype(kind)


def setup_inputs(seed: int = 0) -> dict:
    keys = jax.random.split(jax.random.key(seed), 12)
    lineup_embedding = bell_draw(keys[0], (LINEUP_DEPTH, AMINO_COUNT, LINEUP_WIDTH), 1.0, 6.0, ((0, 4), (1, 8)))
    pair_features = bell_draw(keys[1], (AMINO_COUNT, AMINO_COUNT, CZ), 1.0, 6.0, ((0, 8), (1, 4)))
    lineup_entry_keep = set_ends((jax.random.randint(keys[2], (LINEUP_DEPTH,), 0, 8) < 7).astype(jnp.int32), jax.random.fold_in(keys[2], 1), 0, 1)
    residue_mask = set_ends((jax.random.randint(keys[3], (AMINO_COUNT,), 0, 16) < 15).astype(jnp.int32), jax.random.fold_in(keys[3], 1), 0, 1)
    residue_chain_index = jnp.searchsorted(jnp.cumsum(ragged_sizes(keys[4], 4, AMINO_COUNT, AMINO_COUNT // 2, 0)), jnp.arange(AMINO_COUNT), side="right").astype(jnp.int32)
    intra_chain_bias = bell_draw(keys[5], (HEAD_COUNT,), 1.0, 4.0, (), jnp.float32)
    pair_bias_weight = bell_draw(keys[6], (CZ, HEAD_COUNT), CZ ** -0.5, 0.5)
    attention_weight = draw_attention_weight(jax.random.fold_in(keys[11], 71), 0)
    final_linear_matrix = bell_draw(keys[8], (HEAD_COUNT * HEAD_SPAN, LINEUP_WIDTH), (HEAD_COUNT * HEAD_SPAN) ** -0.5, 0.375)
    tensor_side_matrix = bell_draw(keys[9], (LINEUP_WIDTH, 2 * SIDE_WIDTH), LINEUP_WIDTH ** -0.5, 0.375)
    outer_project_weight = bell_draw(keys[10], (SIDE_WIDTH * SIDE_WIDTH, CZ), SIDE_WIDTH ** -0.5, 1.0)
    return {"lineup_embedding": lineup_embedding, "pair_features": pair_features, "lineup_entry_keep": lineup_entry_keep, "residue_mask": residue_mask, "residue_chain_index": residue_chain_index, "intra_chain_bias": intra_chain_bias, "pair_bias_weight": pair_bias_weight, "attention_weight": attention_weight, "final_linear_matrix": final_linear_matrix, "tensor_side_matrix": tensor_side_matrix, "outer_project_weight": outer_project_weight}


def normalize_layer(values):
    values = values.astype(jnp.float32)
    average = lax.optimization_barrier(jnp.mean(values, axis=-1, keepdims=True))
    centered = values - average
    variance = lax.optimization_barrier(jnp.mean(centered * centered, axis=-1, keepdims=True))
    return centered * lax.rsqrt(variance + 1e-05)

def pair_bias(pair_features, residue_chain_index, intra_chain_bias, pair_bias_weight):
    standardized_embedding = normalize_layer(pair_features).astype(jnp.bfloat16)
    row_total, col_total, channels = standardized_embedding.shape
    biased = jnp.dot(standardized_embedding.reshape(row_total * col_total, channels), pair_bias_weight, preferred_element_type=jnp.float32)
    biased = biased.reshape(row_total, col_total, -1)
    same_chain = (residue_chain_index[:, None] == residue_chain_index[None, :]).astype(jnp.float32)
    biased = biased + same_chain[:, :, None] * intra_chain_bias[None, None, :]
    return jnp.transpose(biased, (2, 0, 1)).astype(jnp.bfloat16)

def row_wise_attention(sequence_rows, combined_bias, key_valid_mask, attention_weight, final_linear_matrix):
    standardized_embedding = normalize_layer(sequence_rows).astype(jnp.bfloat16)
    projected = jnp.dot(standardized_embedding, attention_weight, preferred_element_type=jnp.float32).astype(jnp.bfloat16)
    separated = projected.reshape(AMINO_COUNT, 4, HEAD_COUNT, HEAD_SPAN).astype(jnp.float32)
    queries, key_side, val_side, gate_side = (separated[:, 0], separated[:, 1], separated[:, 2], separated[:, 3])
    scores = jnp.einsum('qhd,khd->hqk', queries, key_side) * (1.0 / HEAD_SPAN ** 0.5)
    scores = scores + combined_bias.astype(jnp.float32) + key_valid_mask[None, None, :]
    maximum = lax.optimization_barrier(jnp.max(scores, axis=-1, keepdims=True))
    expsum = jnp.exp(scores - maximum)
    weights = (expsum / lax.optimization_barrier(jnp.sum(expsum, axis=-1, keepdims=True))).astype(jnp.bfloat16)
    attended = jnp.einsum('hqk,khd->qhd', weights.astype(jnp.float32), val_side)
    gated_rows = (attended * jax.nn.sigmoid(gate_side)).reshape(AMINO_COUNT, HEAD_COUNT * HEAD_SPAN).astype(jnp.bfloat16)
    update = jnp.dot(gated_rows, final_linear_matrix, preferred_element_type=jnp.float32)
    return (sequence_rows.astype(jnp.float32) + update).astype(jnp.bfloat16)

def reference(lineup_embedding, pair_features, lineup_entry_keep, residue_mask, residue_chain_index, intra_chain_bias, pair_bias_weight, attention_weight, final_linear_matrix, tensor_side_matrix, outer_project_weight):
    combined_bias = pair_bias(pair_features, residue_chain_index, intra_chain_bias, pair_bias_weight)
    key_valid_mask = (residue_mask.astype(jnp.float32) - 1.0) * 1000000000.0
    alignment_output = lax.map(lambda sequence_block: row_wise_attention(sequence_block, combined_bias, key_valid_mask, attention_weight, final_linear_matrix), lineup_embedding)
    standardized_embedding = normalize_layer(alignment_output).astype(jnp.bfloat16)
    tensor_sides = jnp.dot(standardized_embedding.reshape(LINEUP_DEPTH * AMINO_COUNT, LINEUP_WIDTH), tensor_side_matrix, preferred_element_type=jnp.float32)
    tensor_sides = tensor_sides.reshape(LINEUP_DEPTH, AMINO_COUNT, 2 * SIDE_WIDTH)
    weight = lineup_entry_keep.astype(jnp.float32)[:, None] * residue_mask.astype(jnp.float32)[None, :]
    tensor_sides = (tensor_sides * weight[:, :, None]).astype(jnp.bfloat16)
    left_side = tensor_sides[:, :, :SIDE_WIDTH]
    right_side = tensor_sides[:, :, SIDE_WIDTH:]
    batch_splitting = N_BRANCH * N_SUB
    members_each_batch = LINEUP_DEPTH // batch_splitting
    row_block = 8
    left_blocks = left_side.reshape(batch_splitting, members_each_batch, AMINO_COUNT // row_block, row_block * SIDE_WIDTH).transpose(2, 0, 1, 3)
    right_flat = right_side.reshape(batch_splitting, members_each_batch, AMINO_COUNT * SIDE_WIDTH).astype(jnp.float32)
    seq_count = jnp.sum(lineup_entry_keep.astype(jnp.float32))
    res_float = residue_mask.astype(jnp.float32)
    denominator = jnp.maximum(seq_count * res_float[:, None] * res_float[None, :], 1.0)
    denom_blocks = denominator.reshape(AMINO_COUNT // row_block, row_block, AMINO_COUNT)

    def one_block(operands):
        left_part, denom_part = operands
        running = jnp.zeros((row_block, AMINO_COUNT, CZ), jnp.float32)
        for group_id in range(batch_splitting):
            outer_sum = jnp.einsum('sa,sb->ab', left_part[group_id].astype(jnp.float32), right_flat[group_id]).astype(jnp.bfloat16)
            arranged = outer_sum.reshape(row_block, SIDE_WIDTH, AMINO_COUNT, SIDE_WIDTH).transpose(0, 2, 1, 3).reshape(row_block * AMINO_COUNT, SIDE_WIDTH * SIDE_WIDTH)
            running = running + jnp.dot(arranged, outer_project_weight, preferred_element_type=jnp.float32).reshape(row_block, AMINO_COUNT, CZ)
        return (running / denom_part[:, :, None]).astype(jnp.bfloat16)
    pair_delta_update = lax.map(one_block, (left_blocks, denom_blocks)).reshape(AMINO_COUNT, AMINO_COUNT, CZ)
    return (alignment_output, pair_delta_update)
```

```python
import jax
import jax.numpy as jnp
from jax import lax
from jax.experimental import pallas as pl
from jax.experimental.pallas import tpu as pltpu
from jax.sharding import PartitionSpec as P

HEAD_COUNT = 8
HEAD_SPAN = 32


def normalize_layer(values):
    values = values.astype(jnp.float32)
    average = jnp.mean(values, axis=-1, keepdims=True)
    centered = values - average
    variance = jnp.mean(centered * centered, axis=-1, keepdims=True)
    return centered * lax.rsqrt(variance + 1e-05)


def pair_bias(pair_features, chain_rows, chain_cols, intra_chain_bias, pair_bias_weight):
    standardized_embedding = normalize_layer(pair_features).astype(jnp.bfloat16)
    row_total, col_total, channels = standardized_embedding.shape
    biased = jnp.dot(
        standardized_embedding.reshape(row_total * col_total, channels),
        pair_bias_weight,
        preferred_element_type=jnp.float32,
    )
    biased = biased.reshape(row_total, col_total, -1)
    same_chain = (chain_rows[:, None] == chain_cols[None, :]).astype(jnp.float32)
    biased = biased + same_chain[:, :, None] * intra_chain_bias[None, None, :]
    return jnp.transpose(biased, (2, 0, 1)).astype(jnp.bfloat16)


def attend(
    row_values,
    normed_keys,
    normed_queries,
    bias,
    key_valid_mask,
    attention_weight,
    final_linear_matrix,
):
    seq_total, key_total, _ = normed_keys.shape
    query_total = normed_queries.shape[1]
    single_head_span = HEAD_COUNT * HEAD_SPAN
    key_values = jnp.einsum(
        "skc,cf->skf",
        normed_keys,
        attention_weight[:, single_head_span : 3 * single_head_span],
        preferred_element_type=jnp.float32,
    ).astype(jnp.bfloat16)
    w_query_gate = jnp.concatenate(
        (attention_weight[:, :single_head_span], attention_weight[:, 3 * single_head_span :]),
        axis=1,
    )
    fronts = jnp.einsum(
        "sqc,cf->sqf", normed_queries, w_query_gate, preferred_element_type=jnp.float32
    ).astype(jnp.bfloat16)
    key_heads = key_values.reshape(seq_total, key_total, 2, HEAD_COUNT, HEAD_SPAN).transpose(
        2, 3, 0, 1, 4
    )
    query_heads = fronts.reshape(seq_total, query_total, 2, HEAD_COUNT, HEAD_SPAN).transpose(
        2, 3, 0, 1, 4
    )
    scaling = 1.0 / HEAD_SPAN**0.5

    def one_head(operands):
        queries, key_side, val_side, bias_head = operands
        scores = jnp.einsum("sqd,skd->sqk", queries, key_side, preferred_element_type=jnp.float32)
        scores = (
            scores * scaling
            + bias_head.astype(jnp.float32)[None, :, :]
            + key_valid_mask[None, None, :]
        )
        maximum = jnp.max(scores, axis=-1, keepdims=True)
        expsum = jnp.exp(scores - maximum)
        weights = (expsum / jnp.sum(expsum, axis=-1, keepdims=True)).astype(jnp.bfloat16)
        return jnp.einsum("sqk,skd->sqd", weights, val_side, preferred_element_type=jnp.float32)

    attended = lax.map(one_head, (query_heads[0], key_heads[0], key_heads[1], bias))
    attended = attended.transpose(1, 2, 0, 3).reshape(seq_total, query_total, single_head_span)
    gate_side = (
        query_heads[1]
        .transpose(1, 2, 0, 3)
        .reshape(seq_total, query_total, single_head_span)
        .astype(jnp.float32)
    )
    gated_rows = (attended * jax.nn.sigmoid(gate_side)).astype(jnp.bfloat16)
    update = jnp.einsum(
        "sqf,fc->sqc", gated_rows, final_linear_matrix, preferred_element_type=jnp.float32
    )
    return (row_values.astype(jnp.float32) + update).astype(jnp.bfloat16)


def attend_whole(
    sequence_rows, combined_bias, key_valid_mask, attention_weight, final_linear_matrix
):
    standardized_embedding = normalize_layer(sequence_rows).astype(jnp.bfloat16)
    return attend(
        sequence_rows,
        standardized_embedding,
        standardized_embedding,
        combined_bias,
        key_valid_mask,
        attention_weight,
        final_linear_matrix,
    )


def outer_product_input(alignment_block, sequence_mask, position_mask, tensor_side_matrix):
    standardized_embedding = normalize_layer(alignment_block).astype(jnp.bfloat16)
    seq_total, res_total, feat_total = standardized_embedding.shape
    values = jnp.dot(
        standardized_embedding.reshape(seq_total * res_total, feat_total),
        tensor_side_matrix,
        preferred_element_type=jnp.float32,
    )
    values = values.reshape(seq_total, res_total, -1)
    weight = sequence_mask.astype(jnp.float32)[:, None] * position_mask.astype(jnp.float32)[None, :]
    return (values * weight[:, :, None]).astype(jnp.bfloat16)


def shards(
    lineup_embedding,
    pair_features,
    lineup_entry_keep,
    residue_mask,
    residue_chain_index,
    intra_chain_bias,
    pair_bias_weight,
    attention_weight,
    final_linear_matrix,
    tensor_side_matrix,
    outer_project_weight,
):
    group_index = lax.axis_index("branch") * lax.axis_size("sub") + lax.axis_index("sub")
    axial_index = lax.axis_index("axial")
    local_res = pair_features.shape[0]
    local_cols = pair_features.shape[1]
    sequence_group = lineup_embedding.shape[0]
    row_start = axial_index * local_res
    col_start = group_index * local_cols
    chain_rows = lax.dynamic_slice_in_dim(residue_chain_index, row_start, local_res)
    chain_cols = lax.dynamic_slice_in_dim(residue_chain_index, col_start, local_cols)
    local_bias = pair_bias(
        pair_features, chain_rows, chain_cols, intra_chain_bias, pair_bias_weight
    )
    key_valid_mask = (residue_mask.astype(jnp.float32) - 1.0) * 1000000000.0
    sequence_rows = lax.all_to_all(
        lineup_embedding, "axial", split_axis=0, concat_axis=1, tiled=True
    )
    partial_bias = lax.all_gather(local_bias, ("branch", "sub"), axis=2, tiled=True)
    combined_bias = lax.all_gather(partial_bias, "axial", axis=1, tiled=True)
    updated = attend_whole(
        sequence_rows, combined_bias, key_valid_mask, attention_weight, final_linear_matrix
    )
    pos_rows = lax.dynamic_slice_in_dim(residue_mask, row_start, local_res)
    pos_cols = lax.dynamic_slice_in_dim(residue_mask, col_start, local_cols)
    back_rows = lax.all_to_all(updated, "axial", split_axis=1, concat_axis=0, tiled=True)
    sequence_mask = lax.dynamic_slice_in_dim(
        lineup_entry_keep, group_index * sequence_group, sequence_group
    )
    factor_rows = outer_product_input(back_rows, sequence_mask, pos_rows, tensor_side_matrix)
    factor_width = factor_rows.shape[2] // 2
    left_flat = factor_rows[:, :, :factor_width].reshape(sequence_group, local_res * factor_width)
    right_all = lax.all_gather(factor_rows[:, :, factor_width:], "axial", axis=1, tiled=True)
    row_count = lax.axis_size(("branch", "sub")) * local_cols
    chosen = right_all
    chosen = chosen.reshape(sequence_group, row_count * factor_width)
    outer_sum = lax.dot_general(
        left_flat, chosen, (((0,), (0,)), ((), ())), preferred_element_type=jnp.float32
    )
    outer_sum = outer_sum.astype(jnp.bfloat16)
    arranged = outer_sum.reshape(local_res, factor_width, row_count, factor_width).transpose(
        2, 0, 1, 3
    )
    arranged = arranged.reshape(row_count * local_res, factor_width * factor_width)
    opm_total = lax.psum_scatter(
        jnp.dot(arranged, outer_project_weight, preferred_element_type=jnp.float32).reshape(
            row_count, local_res, -1
        ),
        ("branch", "sub"),
        scatter_dimension=0,
        tiled=True,
    )
    pair_sums = jnp.transpose(opm_total, (1, 0, 2))
    seq_count = jnp.sum(lineup_entry_keep.astype(jnp.float32))
    counted = (
        seq_count * pos_rows.astype(jnp.float32)[:, None] * pos_cols.astype(jnp.float32)[None, :]
    )
    pair_delta_update = (pair_sums / jnp.maximum(counted, 1.0)[:, :, None]).astype(jnp.bfloat16)
    return (back_rows, pair_delta_update)


def iota(shape, dim):
    return lax.broadcasted_iota(jnp.int32, shape, dim)


def mm(a, b):
    return jnp.dot(a, b, preferred_element_type=jnp.float32)


def mm_t(a, b):
    return lax.dot_general(a, b, (((1,), (1,)), ((), ())), preferred_element_type=jnp.float32)


def one_hot(cond):
    return jnp.where(cond, 1.0, 0.0).astype(jnp.bfloat16)


def pick_lanes(cond, row):
    return jnp.sum(jnp.where(cond, row, 0.0), axis=-1, keepdims=True)


def fused_kernel(
    own_ref,
    pair_ref,
    keep_ref,
    mask_ref,
    chain_ref,
    intra_ref,
    pbw_ref,
    aw_hbm,
    fw_hbm,
    tw_hbm,
    pw_hbm,
    out_ref,
    pair_out_ref,
    msa,
    bias_part,
    bias_all,
    aligned,
    normed,
    partial,
    landed,
    aw,
    fw,
    tw,
    pw,
    aw_t,
    left_w,
    right_w,
    load_sem,
    msa_send,
    msa_recv,
    part_send,
    part_recv,
    all_send,
    all_recv,
    sum_send,
    sum_recv,
):
    f32, bf16 = jnp.float32, jnp.bfloat16
    axial = lax.axis_index("axial")
    n_axial = lax.axis_size("axial")
    n_sub = lax.axis_size("sub")
    group = lax.axis_index("branch") * n_sub + lax.axis_index("sub")
    n_group = lax.axis_size("branch") * n_sub
    axial_peers = [lax.rem(axial + d, n_axial) for d in range(n_axial)]
    group_peers = [lax.rem(group + d, n_group) for d in range(n_group)]

    def axial_id(d):
        return {"axial": axial_peers[d]}

    def group_id(d):
        return {"branch": group_peers[d] // n_sub, "sub": group_peers[d] % n_sub}

    barrier = pltpu.get_barrier_semaphore()
    for d in range(1, n_axial):
        pl.semaphore_signal(barrier, 1, device_id=axial_id(d), device_id_type=pl.DeviceIdType.MESH)
    for d in range(1, n_group):
        pl.semaphore_signal(barrier, 1, device_id=group_id(d), device_id_type=pl.DeviceIdType.MESH)
    loads = [
        pltpu.make_async_copy(src, dst, load_sem.at[n])
        for n, (src, dst) in enumerate(((aw_hbm, aw), (fw_hbm, fw), (tw_hbm, tw), (pw_hbm, pw)))
    ]
    for load in loads:
        load.start()

    pair_rows = normalize_layer(pair_ref[...])
    padded = jnp.concatenate([pair_rows] * 4, axis=0).astype(bf16)
    local = mm(padded, pbw_ref[...]).T
    lane = iota((32, 128), 1)
    chain = jnp.broadcast_to(chain_ref[...].astype(f32), (8, 32)).astype(bf16)
    chain_i = mm(chain, one_hot(iota((32, 128), 0) == axial * 4 + ((lane >> 3) & 3)))
    chain_j = mm(chain, one_hot(iota((32, 128), 0) == group * 8 + (lane & 7)))
    head_row = iota((8, 128), 0)
    intra = jnp.zeros((8, 128), f32)
    for h in range(HEAD_COUNT):
        intra = jnp.where(head_row == h, intra_ref[h], intra)
    local = local + jnp.where(chain_i == chain_j, intra, 0.0)
    local = local.astype(bf16).astype(f32)
    local = jnp.where((iota((8, 128), 1) >> 5) == group, local, 0.0)
    bias_part[0] = local
    msa[:, axial] = own_ref[...]

    pl.semaphore_wait(barrier, n_axial + n_group - 2)
    sends = []
    for d in range(1, n_group):
        copy = pltpu.make_async_remote_copy(
            bias_part.at[0], bias_part.at[d], part_send.at[d], part_recv.at[d],
            device_id=group_id(d), device_id_type=pl.DeviceIdType.MESH,
        )
        copy.start()
        sends.append(copy)
    part_copies = list(sends)
    msa_copies = []
    for d in range(1, n_axial):
        copy = pltpu.make_async_remote_copy(
            own_ref, msa.at[:, axial], msa_send.at[d], msa_recv.at[d],
            device_id=axial_id(d), device_id_type=pl.DeviceIdType.MESH,
        )
        copy.start()
        sends.append(copy)
        msa_copies.append(copy)

    keep = keep_ref[...].astype(f32)
    mask = mask_ref[...].astype(f32)
    row = iota((256, 32), 0)
    lane32 = iota((256, 32), 1)
    row_mask = pick_lanes(lane32 == ((row >> 4) & 7) * 4 + (row & 3), mask)
    row_keep = pick_lanes(lane32 == group * 8 + (row >> 7) * 4 + ((row >> 2) & 3), keep)
    row_weight = row_keep * row_mask
    key_mask = (row_mask[:128] - 1.0) * 1000000000.0
    seq_count = jnp.sum(keep)
    for part in range(1, n_group):
        part_copies[part - 1].wait_recv()
    combined = bias_part[0]
    for part in range(1, n_group):
        combined = combined + bias_part[part]
    bias_all[axial] = combined
    all_copies = []
    for d in range(1, n_axial):
        copy = pltpu.make_async_remote_copy(
            bias_all.at[axial], bias_all.at[axial], all_send.at[d], all_recv.at[d],
            device_id=axial_id(d), device_id_type=pl.DeviceIdType.MESH,
        )
        copy.start()
        sends.append(copy)
        all_copies.append(copy)

    for load in loads:
        load.wait()
    for n, at in enumerate((0, 2, 3)):
        aw_t[n * 256 : (n + 1) * 256, :] = aw[:, at * 256 : (at + 1) * 256].T
    side = tw[...]
    lanes = iota((64, 1024), 1)
    left_w[...] = mm(side, one_hot(iota((64, 1024), 0) == (lanes >> 5))).astype(bf16)
    right_w[...] = mm(side, one_hot(iota((64, 1024), 0) == 32 + (lanes & 31))).astype(bf16)
    k_at, c_at = iota((128, 128), 0), iota((128, 128), 1)
    key_pick = one_hot((k_at >> 4) * 4 + (k_at & 3) == (c_at >> 5) * 8 + (c_at & 7))
    query_pick = ((c_at >> 3) & 3) == (k_at & 3)
    same_sequence = ((k_at >> 2) & 3) == ((c_at >> 2) & 3)

    for copy in msa_copies:
        copy.wait_recv()
    rows = msa[...].reshape(256, 256)
    rows_normed = normalize_layer(rows).astype(bf16)
    keys = mm(rows_normed, aw[:, 256:512]).astype(bf16)
    fronts = mm_t(aw_t[...], rows_normed).astype(bf16)
    gate_t = jax.nn.sigmoid(fronts[512:].astype(f32))

    for copy in all_copies:
        copy.wait_recv()
    scaling = 1.0 / HEAD_SPAN**0.5
    attended = [[], []]
    for h in range(HEAD_COUNT):
        spread = jnp.concatenate(
            [jnp.broadcast_to(bias_all[a, h : h + 1, :], (16, 128)) for a in range(8)], axis=0
        )
        spread = jnp.where(query_pick, spread, 0.0).astype(bf16)
        bias = jnp.where(same_sequence, mm_t(key_pick, spread), -1e30)
        lo, hi = h * HEAD_SPAN, (h + 1) * HEAD_SPAN
        for half in range(2):
            at = slice(half * 128, (half + 1) * 128)
            pieces = [fronts[lo:hi, at]]
            if lo:
                pieces.insert(0, jnp.zeros((lo, 128), bf16))
            if hi < 256:
                pieces.append(jnp.zeros((256 - hi, 128), bf16))
            scores = mm(keys[at], jnp.concatenate(pieces, axis=0)) * scaling + bias + key_mask
            raised = jnp.exp(scores - jnp.max(scores, axis=0, keepdims=True))
            weights = raised * (1.0 / jnp.sum(raised, axis=0, keepdims=True))
            attended[half].append(mm(fronts[256 + lo : 256 + hi, at], weights.astype(bf16)))
    attended_t = jnp.concatenate(
        [jnp.concatenate(attended[half], axis=0) for half in range(2)], axis=1
    )
    gated = (attended_t * gate_t).T.astype(bf16)
    updated = (rows.astype(f32) + mm(gated, fw[...])).astype(bf16)
    aligned[...] = updated.reshape(2, 8, 16, 256)
    out_ref[...] = aligned[:, axial]
    side_in = (normalize_layer(updated) * row_weight).astype(bf16)
    normed[...] = side_in.reshape(2, 8, 16, 256)

    own_side = normed[:, axial].reshape(32, 256)
    r_at = iota((128, 32), 0)
    own_pick = one_hot(iota((128, 32), 1) == ((r_at >> 2) & 7) * 4 + (r_at >> 5))
    own_spread = mm(own_pick, own_side).astype(bf16)
    projected = jnp.zeros((256, 128), f32)
    for chunk in range(4):
        at = slice(chunk * 256, (chunk + 1) * 256)
        right = mm(side_in, right_w[:, at]).astype(bf16).astype(f32).reshape(2, 8, 2, 8, 256)
        left = mm(own_spread, left_w[:, at]).astype(bf16).astype(f32).reshape(4, 2, 2, 8, 256)
        outer = []
        for i in range(4):
            total = right[0, :, 0] * left[i, 0, 0][None]
            for half, two in ((0, 1), (1, 0), (1, 1)):
                total = total + right[half, :, two] * left[i, half, two][None]
            outer.append(total.reshape(64, 256))
        projected = projected + mm(jnp.concatenate(outer, axis=0).astype(bf16), pw[at, :])
    tiles = projected.reshape(4, 8, 8, 128)
    upper = iota((8, 128), 0) < 4
    for g in range(4):
        for i in range(4):
            one, two = tiles[i, 2 * g], tiles[i, 2 * g + 1]
            one = one + pltpu.roll(one, 4, 0)
            two = two + pltpu.roll(two, 4, 0)
            partial[g, i] = jnp.where(upper, one, two)
    sum_copies = []
    for d in range(1, n_group):
        copy = pltpu.make_async_remote_copy(
            partial.at[group_peers[d]], landed.at[d], sum_send.at[d], sum_recv.at[d],
            device_id=group_id(d), device_id_type=pl.DeviceIdType.MESH,
        )
        copy.start()
        sends.append(copy)
        sum_copies.append(copy)
    small_lane = iota((8, 32), 1)
    col_mask = pick_lanes(small_lane == group * 8 + iota((8, 32), 0), mask)
    counts = [
        jnp.maximum(seq_count * pick_lanes(small_lane == axial * 4 + i, mask) * col_mask, 1.0)
        for i in range(4)
    ]
    for copy in sum_copies:
        copy.wait_recv()
    total = partial[group] + landed[1] + landed[2] + landed[3]
    for i in range(4):
        pair_out_ref[i] = (total[i] / counts[i]).astype(bf16)
    for copy in sends:
        copy.wait_send()


def fused(lineup, pair, keep, mask, chain, intra, pbw, aw, fw, tw, pw):
    f32, bf16 = jnp.float32, jnp.bfloat16
    vmem = pl.BlockSpec(memory_space=pltpu.VMEM)
    anywhere = pl.BlockSpec(memory_space=pl.ANY)
    dma = pltpu.SemaphoreType.DMA
    out, pair_out = pl.pallas_call(
        fused_kernel,
        out_shape=(
            jax.ShapeDtypeStruct((2, 16, 256), bf16),
            jax.ShapeDtypeStruct((4, 8, 128), bf16),
        ),
        in_specs=[vmem] * 5 + [pl.BlockSpec(memory_space=pltpu.SMEM), vmem] + [anywhere] * 4,
        out_specs=(vmem, vmem),
        scratch_shapes=[
            pltpu.VMEM((2, 8, 16, 256), bf16),
            pltpu.VMEM((4, 8, 128), f32),
            pltpu.VMEM((8, 8, 128), f32),
            pltpu.VMEM((2, 8, 16, 256), bf16),
            pltpu.VMEM((2, 8, 16, 256), bf16),
            pltpu.VMEM((4, 4, 8, 128), f32),
            pltpu.VMEM((4, 4, 8, 128), f32),
            pltpu.VMEM(aw.shape, bf16),
            pltpu.VMEM(fw.shape, bf16),
            pltpu.VMEM(tw.shape, bf16),
            pltpu.VMEM(pw.shape, bf16),
            pltpu.VMEM((768, 256), bf16),
            pltpu.VMEM((256, 1024), bf16),
            pltpu.VMEM((256, 1024), bf16),
            dma((4,)),
            dma((8,)), dma((8,)),
            dma((4,)), dma((4,)),
            dma((8,)), dma((8,)),
            dma((4,)), dma((4,)),
        ],
        compiler_params=pltpu.CompilerParams(
            collective_id=0, has_side_effects=True, vmem_limit_bytes=32 * 1024 * 1024
        ),
    )(
        lineup.reshape(2, 16, 256),
        pair.reshape(32, 128),
        keep.reshape(1, 32),
        mask.reshape(1, 32),
        chain.reshape(1, 32),
        intra,
        pbw,
        aw,
        fw,
        tw,
        pw,
    )
    return out.reshape(lineup.shape), pair_out


def per_device(lineup, pair, *rest):
    axial, groups = lax.axis_size("axial"), lax.axis_size(("branch", "sub"))
    small = lineup.shape == (8, 4, 256) and pair.shape == (4, 8, 128)
    body = fused if small and axial == 8 and groups == 4 else shards
    return body(lineup, pair, *rest)


def solution(mesh):
    in_specs = (
        P(("branch", "sub"), "axial", None),
        P("axial", ("branch", "sub"), None),
        P(),
        P(),
        P(),
        P(),
        P(),
        P(),
        P(),
        P(),
        P(),
    )
    out_specs = (P(("branch", "sub"), "axial", None), P("axial", ("branch", "sub"), None))
    return jax.shard_map(
        per_device, mesh=mesh, in_specs=in_specs, out_specs=out_specs, check_vma=False
    )
```

```python
import jax
import jax.numpy as jnp
from jax import lax
from jax.experimental import pallas as pl
from jax.experimental.pallas import tpu as pltpu
from jax.sharding import PartitionSpec as P

HEAD_COUNT = 8
HEAD_SPAN = 32


def normalize_layer(values):
    values = values.astype(jnp.float32)
    average = jnp.mean(values, axis=-1, keepdims=True)
    centered = values - average
    variance = jnp.mean(centered * centered, axis=-1, keepdims=True)
    return centered * lax.rsqrt(variance + 1e-05)


def pair_bias(pair_features, chain_rows, chain_cols, intra_chain_bias, pair_bias_weight):
    standardized_embedding = normalize_layer(pair_features).astype(jnp.bfloat16)
    row_total, col_total, channels = standardized_embedding.shape
    biased = jnp.dot(
        standardized_embedding.reshape(row_total * col_total, channels),
        pair_bias_weight,
        preferred_element_type=jnp.float32,
    )
    biased = biased.reshape(row_total, col_total, -1)
    same_chain = (chain_rows[:, None] == chain_cols[None, :]).astype(jnp.float32)
    biased = biased + same_chain[:, :, None] * intra_chain_bias[None, None, :]
    return jnp.transpose(biased, (2, 0, 1)).astype(jnp.bfloat16)


def attend(
    row_values,
    normed_keys,
    normed_queries,
    bias,
    key_valid_mask,
    attention_weight,
    final_linear_matrix,
):
    seq_total, key_total, _ = normed_keys.shape
    query_total = normed_queries.shape[1]
    single_head_span = HEAD_COUNT * HEAD_SPAN
    key_values = jnp.einsum(
        "skc,cf->skf",
        normed_keys,
        attention_weight[:, single_head_span : 3 * single_head_span],
        preferred_element_type=jnp.float32,
    ).astype(jnp.bfloat16)
    w_query_gate = jnp.concatenate(
        (attention_weight[:, :single_head_span], attention_weight[:, 3 * single_head_span :]),
        axis=1,
    )
    fronts = jnp.einsum(
        "sqc,cf->sqf", normed_queries, w_query_gate, preferred_element_type=jnp.float32
    ).astype(jnp.bfloat16)
    key_heads = key_values.reshape(seq_total, key_total, 2, HEAD_COUNT, HEAD_SPAN).transpose(
        2, 3, 0, 1, 4
    )
    query_heads = fronts.reshape(seq_total, query_total, 2, HEAD_COUNT, HEAD_SPAN).transpose(
        2, 3, 0, 1, 4
    )
    scaling = 1.0 / HEAD_SPAN**0.5

    def one_head(operands):
        queries, key_side, val_side, bias_head = operands
        scores = jnp.einsum("sqd,skd->sqk", queries, key_side, preferred_element_type=jnp.float32)
        scores = (
            scores * scaling
            + bias_head.astype(jnp.float32)[None, :, :]
            + key_valid_mask[None, None, :]
        )
        maximum = jnp.max(scores, axis=-1, keepdims=True)
        expsum = jnp.exp(scores - maximum)
        weights = (expsum / jnp.sum(expsum, axis=-1, keepdims=True)).astype(jnp.bfloat16)
        return jnp.einsum("sqk,skd->sqd", weights, val_side, preferred_element_type=jnp.float32)

    attended = lax.map(one_head, (query_heads[0], key_heads[0], key_heads[1], bias))
    attended = attended.transpose(1, 2, 0, 3).reshape(seq_total, query_total, single_head_span)
    gate_side = (
        query_heads[1]
        .transpose(1, 2, 0, 3)
        .reshape(seq_total, query_total, single_head_span)
        .astype(jnp.float32)
    )
    gated_rows = (attended * jax.nn.sigmoid(gate_side)).astype(jnp.bfloat16)
    update = jnp.einsum(
        "sqf,fc->sqc", gated_rows, final_linear_matrix, preferred_element_type=jnp.float32
    )
    return (row_values.astype(jnp.float32) + update).astype(jnp.bfloat16)


def attend_whole(
    sequence_rows, combined_bias, key_valid_mask, attention_weight, final_linear_matrix
):
    standardized_embedding = normalize_layer(sequence_rows).astype(jnp.bfloat16)
    return attend(
        sequence_rows,
        standardized_embedding,
        standardized_embedding,
        combined_bias,
        key_valid_mask,
        attention_weight,
        final_linear_matrix,
    )


def outer_product_input(alignment_block, sequence_mask, position_mask, tensor_side_matrix):
    standardized_embedding = normalize_layer(alignment_block).astype(jnp.bfloat16)
    seq_total, res_total, feat_total = standardized_embedding.shape
    values = jnp.dot(
        standardized_embedding.reshape(seq_total * res_total, feat_total),
        tensor_side_matrix,
        preferred_element_type=jnp.float32,
    )
    values = values.reshape(seq_total, res_total, -1)
    weight = sequence_mask.astype(jnp.float32)[:, None] * position_mask.astype(jnp.float32)[None, :]
    return (values * weight[:, :, None]).astype(jnp.bfloat16)


def shards(
    lineup_embedding,
    pair_features,
    lineup_entry_keep,
    residue_mask,
    residue_chain_index,
    intra_chain_bias,
    pair_bias_weight,
    attention_weight,
    final_linear_matrix,
    tensor_side_matrix,
    outer_project_weight,
):
    group_index = lax.axis_index("branch") * lax.axis_size("sub") + lax.axis_index("sub")
    axial_index = lax.axis_index("axial")
    local_res = pair_features.shape[0]
    local_cols = pair_features.shape[1]
    sequence_group = lineup_embedding.shape[0]
    row_start = axial_index * local_res
    col_start = group_index * local_cols
    chain_rows = lax.dynamic_slice_in_dim(residue_chain_index, row_start, local_res)
    chain_cols = lax.dynamic_slice_in_dim(residue_chain_index, col_start, local_cols)
    local_bias = pair_bias(
        pair_features, chain_rows, chain_cols, intra_chain_bias, pair_bias_weight
    )
    key_valid_mask = (residue_mask.astype(jnp.float32) - 1.0) * 1000000000.0
    sequence_rows = lax.all_to_all(
        lineup_embedding, "axial", split_axis=0, concat_axis=1, tiled=True
    )
    partial_bias = lax.all_gather(local_bias, ("branch", "sub"), axis=2, tiled=True)
    combined_bias = lax.all_gather(partial_bias, "axial", axis=1, tiled=True)
    updated = attend_whole(
        sequence_rows, combined_bias, key_valid_mask, attention_weight, final_linear_matrix
    )
    pos_rows = lax.dynamic_slice_in_dim(residue_mask, row_start, local_res)
    pos_cols = lax.dynamic_slice_in_dim(residue_mask, col_start, local_cols)
    back_rows = lax.all_to_all(updated, "axial", split_axis=1, concat_axis=0, tiled=True)
    sequence_mask = lax.dynamic_slice_in_dim(
        lineup_entry_keep, group_index * sequence_group, sequence_group
    )
    factor_rows = outer_product_input(back_rows, sequence_mask, pos_rows, tensor_side_matrix)
    factor_width = factor_rows.shape[2] // 2
    left_flat = factor_rows[:, :, :factor_width].reshape(sequence_group, local_res * factor_width)
    right_all = lax.all_gather(factor_rows[:, :, factor_width:], "axial", axis=1, tiled=True)
    row_count = lax.axis_size(("branch", "sub")) * local_cols
    chosen = right_all
    chosen = chosen.reshape(sequence_group, row_count * factor_width)
    outer_sum = lax.dot_general(
        left_flat, chosen, (((0,), (0,)), ((), ())), preferred_element_type=jnp.float32
    )
    outer_sum = outer_sum.astype(jnp.bfloat16)
    arranged = outer_sum.reshape(local_res, factor_width, row_count, factor_width).transpose(
        2, 0, 1, 3
    )
    arranged = arranged.reshape(row_count * local_res, factor_width * factor_width)
    opm_total = lax.psum_scatter(
        jnp.dot(arranged, outer_project_weight, preferred_element_type=jnp.float32).reshape(
            row_count, local_res, -1
        ),
        ("branch", "sub"),
        scatter_dimension=0,
        tiled=True,
    )
    pair_sums = jnp.transpose(opm_total, (1, 0, 2))
    seq_count = jnp.sum(lineup_entry_keep.astype(jnp.float32))
    counted = (
        seq_count * pos_rows.astype(jnp.float32)[:, None] * pos_cols.astype(jnp.float32)[None, :]
    )
    pair_delta_update = (pair_sums / jnp.maximum(counted, 1.0)[:, :, None]).astype(jnp.bfloat16)
    return (back_rows, pair_delta_update)


def iota(shape, dim):
    return lax.broadcasted_iota(jnp.int32, shape, dim)


def mm(a, b):
    return jnp.dot(a, b, preferred_element_type=jnp.float32)


def mm_t(a, b):
    return lax.dot_general(a, b, (((1,), (1,)), ((), ())), preferred_element_type=jnp.float32)


def one_hot(cond):
    return jnp.where(cond, 1.0, 0.0).astype(jnp.bfloat16)


def pick_lanes(cond, row):
    return jnp.sum(jnp.where(cond, row, 0.0), axis=-1, keepdims=True)


def fused_kernel(
    own_hbm,
    pair_hbm,
    keep_hbm,
    mask_hbm,
    chain_hbm,
    intra_hbm,
    pbw_hbm,
    aw_hbm,
    fw_hbm,
    tw_hbm,
    pw_hbm,
    out_ref,
    pair_out_ref,
    own_ref,
    pair_ref,
    keep_ref,
    mask_ref,
    chain_ref,
    intra_ref,
    pbw_ref,
    msa,
    bias_part,
    bias_all,
    aligned,
    normed,
    partial,
    landed,
    aw,
    fw,
    tw,
    pw,
    aw_t,
    left_w,
    right_w,
    load_sem,
    msa_send,
    msa_recv,
    part_send,
    part_recv,
    all_send,
    all_recv,
    sum_send,
    sum_recv,
):
    f32, bf16 = jnp.float32, jnp.bfloat16
    axial = lax.axis_index("axial")
    n_axial = lax.axis_size("axial")
    n_sub = lax.axis_size("sub")
    group = lax.axis_index("branch") * n_sub + lax.axis_index("sub")
    n_group = lax.axis_size("branch") * n_sub
    axial_peers = [lax.rem(axial + d, n_axial) for d in range(n_axial)]
    group_peers = [lax.rem(group + d, n_group) for d in range(n_group)]

    def axial_id(d):
        return {"axial": axial_peers[d]}

    def group_id(d):
        return {"branch": group_peers[d] // n_sub, "sub": group_peers[d] % n_sub}

    loads = [
        pltpu.make_async_copy(src, dst, load_sem.at[n])
        for n, (src, dst) in enumerate(
            (
                (pair_hbm, pair_ref),
                (pbw_hbm, pbw_ref),
                (chain_hbm, chain_ref),
                (intra_hbm, intra_ref),
                (own_hbm, own_ref),
                (keep_hbm, keep_ref),
                (mask_hbm, mask_ref),
                (aw_hbm, aw),
                (tw_hbm, tw),
                (fw_hbm, fw),
                (pw_hbm, pw),
            )
        )
    ]
    for load in loads[:5]:
        load.start()
    barrier = pltpu.get_barrier_semaphore()
    for d in range(1, n_axial):
        pl.semaphore_signal(barrier, 1, device_id=axial_id(d), device_id_type=pl.DeviceIdType.MESH)
    for d in range(1, n_group):
        pl.semaphore_signal(barrier, 1, device_id=group_id(d), device_id_type=pl.DeviceIdType.MESH)
    for load in loads[5:]:
        load.start()
    for load in loads[:5]:
        load.wait()

    pair_rows = normalize_layer(pair_ref[...])
    padded = jnp.concatenate([pair_rows] * 4, axis=0).astype(bf16)
    local = mm_t(pbw_ref[...], padded)
    lane = iota((32, 128), 1)
    chain = jnp.broadcast_to(chain_ref[...].astype(f32), (8, 32)).astype(bf16)
    chain_i = mm(chain, one_hot(iota((32, 128), 0) == axial * 4 + ((lane >> 3) & 3)))
    chain_j = mm(chain, one_hot(iota((32, 128), 0) == group * 8 + (lane & 7)))
    head_row = iota((8, 128), 0)
    intra = jnp.zeros((8, 128), f32)
    for h in range(HEAD_COUNT):
        intra = jnp.where(head_row == h, intra_ref[h], intra)
    local = local + jnp.where(chain_i == chain_j, intra, 0.0)
    local = local.astype(bf16).astype(f32)
    local = jnp.where((iota((8, 128), 1) >> 5) == group, local, 0.0)
    bias_part[0] = local
    msa[:, axial] = own_ref[...].astype(f32).reshape(2, 16, 256).astype(bf16)

    pl.semaphore_wait(barrier, n_axial + n_group - 2)
    sends = []
    for d in range(1, n_group):
        copy = pltpu.make_async_remote_copy(
            bias_part.at[0], bias_part.at[d], part_send.at[d], part_recv.at[d],
            device_id=group_id(d), device_id_type=pl.DeviceIdType.MESH,
        )
        copy.start()
        sends.append(copy)
    part_copies = list(sends)
    msa_copies = []
    for d in range(1, n_axial):
        copy = pltpu.make_async_remote_copy(
            msa.at[:, axial], msa.at[:, axial], msa_send.at[d], msa_recv.at[d],
            device_id=axial_id(d), device_id_type=pl.DeviceIdType.MESH,
        )
        copy.start()
        sends.append(copy)
        msa_copies.append(copy)

    for load in loads[5:7]:
        load.wait()
    keep = keep_ref[...].astype(f32)
    mask = mask_ref[...].astype(f32)
    row = iota((256, 32), 0)
    lane32 = iota((256, 32), 1)
    row_mask = pick_lanes(lane32 == ((row >> 4) & 7) * 4 + (row & 3), mask)
    row_keep = pick_lanes(lane32 == group * 8 + (row >> 7) * 4 + ((row >> 2) & 3), keep)
    row_weight = row_keep * row_mask
    key_mask = (row_mask[:128] - 1.0) * 1000000000.0
    seq_count = jnp.sum(keep)
    for part in range(1, n_group):
        part_copies[part - 1].wait_recv()
    combined = bias_part[0]
    for part in range(1, n_group):
        combined = combined + bias_part[part]
    bias_all[axial] = combined
    all_copies = []
    for d in range(1, n_axial):
        copy = pltpu.make_async_remote_copy(
            bias_all.at[axial], bias_all.at[axial], all_send.at[d], all_recv.at[d],
            device_id=axial_id(d), device_id_type=pl.DeviceIdType.MESH,
        )
        copy.start()
        sends.append(copy)
        all_copies.append(copy)

    for load in loads[7:]:
        load.wait()
    for n, at in enumerate((0, 2, 3)):
        aw_t[n * 256 : (n + 1) * 256, :] = aw[:, at * 256 : (at + 1) * 256].T
    side = tw[...]
    rank, channel = iota((1024, 64), 0), iota((1024, 64), 1)
    left_w[...] = mm(one_hot(channel == (rank >> 5)), side).astype(bf16)
    right_w[...] = mm(one_hot(channel == 32 + (rank & 31)), side).astype(bf16)
    k_at, c_at = iota((128, 128), 0), iota((128, 128), 1)
    key_pick = one_hot((k_at >> 4) * 4 + (k_at & 3) == (c_at >> 5) * 8 + (c_at & 7))
    query_pick = ((c_at >> 3) & 3) == (k_at & 3)
    same_sequence = ((k_at >> 2) & 3) == ((c_at >> 2) & 3)

    for copy in msa_copies:
        copy.wait_recv()
    rows = msa[...].reshape(256, 256)
    rows_normed = normalize_layer(rows).astype(bf16)
    keys = mm(rows_normed, aw[:, 256:512]).astype(bf16)
    fronts = mm_t(aw_t[...], rows_normed).astype(bf16)
    gate_t = jax.nn.sigmoid(fronts[512:].astype(f32))

    for copy in all_copies:
        copy.wait_recv()
    scaling = 1.0 / HEAD_SPAN**0.5
    attended = [[], []]
    for h in range(HEAD_COUNT):
        spread = jnp.concatenate(
            [jnp.broadcast_to(bias_all[a, h : h + 1, :], (16, 128)) for a in range(8)], axis=0
        )
        spread = jnp.where(query_pick, spread, 0.0).astype(bf16)
        bias = jnp.where(same_sequence, mm_t(key_pick, spread), -1e30)
        lo, hi = h * HEAD_SPAN, (h + 1) * HEAD_SPAN
        for half in range(2):
            at = slice(half * 128, (half + 1) * 128)
            pieces = [fronts[lo:hi, at]]
            if lo:
                pieces.insert(0, jnp.zeros((lo, 128), bf16))
            if hi < 256:
                pieces.append(jnp.zeros((256 - hi, 128), bf16))
            scores = mm(keys[at], jnp.concatenate(pieces, axis=0)) * scaling + bias + key_mask
            raised = jnp.exp(scores - jnp.max(scores, axis=0, keepdims=True))
            weights = raised * (1.0 / jnp.sum(raised, axis=0, keepdims=True))
            attended[half].append(mm(fronts[256 + lo : 256 + hi, at], weights.astype(bf16)))
    attended_t = jnp.concatenate(
        [jnp.concatenate(attended[half], axis=0) for half in range(2)], axis=1
    )
    gated = (attended_t * gate_t).T.astype(bf16)
    updated = (rows.astype(f32) + mm(gated, fw[...])).astype(bf16)
    aligned[...] = updated.reshape(2, 8, 16, 256)
    out_ref[...] = aligned[:, axial].astype(f32).reshape(8, 4, 256).astype(bf16)
    side_in = (normalize_layer(updated) * row_weight).astype(bf16)
    normed[...] = side_in.reshape(2, 8, 16, 256)

    own_side = normed[:, axial].reshape(32, 256)
    r_at = iota((128, 32), 0)
    own_pick = one_hot(iota((128, 32), 1) == ((r_at >> 2) & 7) * 4 + (r_at >> 5))
    own_spread = mm(own_pick, own_side).astype(bf16)
    projected = jnp.zeros((256, 128), f32)
    for chunk in range(4):
        at = slice(chunk * 256, (chunk + 1) * 256)
        right = mm_t(side_in, right_w[at]).astype(bf16).astype(f32).reshape(2, 8, 2, 8, 256)
        left = mm_t(own_spread, left_w[at]).astype(bf16).astype(f32).reshape(4, 2, 2, 8, 256)
        outer = []
        for i in range(4):
            total = right[0, :, 0] * left[i, 0, 0][None]
            for half, two in ((0, 1), (1, 0), (1, 1)):
                total = total + right[half, :, two] * left[i, half, two][None]
            outer.append(total.reshape(64, 256))
        projected = projected + mm(jnp.concatenate(outer, axis=0).astype(bf16), pw[at, :])
    tiles = projected.reshape(4, 8, 8, 128)
    upper = iota((8, 128), 0) < 4
    for g in range(4):
        for i in range(4):
            one, two = tiles[i, 2 * g], tiles[i, 2 * g + 1]
            one = one + pltpu.roll(one, 4, 0)
            two = two + pltpu.roll(two, 4, 0)
            partial[g, i] = jnp.where(upper, one, two)
    sum_copies = []
    for d in range(1, n_group):
        copy = pltpu.make_async_remote_copy(
            partial.at[group_peers[d]], landed.at[d], sum_send.at[d], sum_recv.at[d],
            device_id=group_id(d), device_id_type=pl.DeviceIdType.MESH,
        )
        copy.start()
        sends.append(copy)
        sum_copies.append(copy)
    small_lane = iota((8, 32), 1)
    col_mask = pick_lanes(small_lane == group * 8 + iota((8, 32), 0), mask)
    counts = [
        jnp.maximum(seq_count * pick_lanes(small_lane == axial * 4 + i, mask) * col_mask, 1.0)
        for i in range(4)
    ]
    for copy in sum_copies:
        copy.wait_recv()
    total = partial[group] + landed[1] + landed[2] + landed[3]
    for i in range(4):
        pair_out_ref[i] = (total[i] / counts[i]).astype(bf16)
    for copy in sends:
        copy.wait_send()


def fused(lineup, pair, keep, mask, chain, intra, pbw, aw, fw, tw, pw):
    f32, bf16 = jnp.float32, jnp.bfloat16
    vmem = pl.BlockSpec(memory_space=pltpu.VMEM)
    hbm = pl.BlockSpec(memory_space=pltpu.HBM)
    dma = pltpu.SemaphoreType.DMA
    out, pair_out = pl.pallas_call(
        fused_kernel,
        out_shape=(
            jax.ShapeDtypeStruct(lineup.shape, bf16),
            jax.ShapeDtypeStruct((4, 8, 128), bf16),
        ),
        in_specs=[hbm] * 11,
        out_specs=(vmem, vmem),
        scratch_shapes=[
            pltpu.VMEM(lineup.shape, bf16),
            pltpu.VMEM((32, 128), bf16),
            pltpu.VMEM((1, 32), jnp.int32),
            pltpu.VMEM((1, 32), jnp.int32),
            pltpu.VMEM((1, 32), jnp.int32),
            pltpu.SMEM((HEAD_COUNT,), f32),
            pltpu.VMEM((HEAD_COUNT, 128), bf16),
            pltpu.VMEM((2, 8, 16, 256), bf16),
            pltpu.VMEM((4, 8, 128), f32),
            pltpu.VMEM((8, 8, 128), f32),
            pltpu.VMEM((2, 8, 16, 256), bf16),
            pltpu.VMEM((2, 8, 16, 256), bf16),
            pltpu.VMEM((4, 4, 8, 128), f32),
            pltpu.VMEM((4, 4, 8, 128), f32),
            pltpu.VMEM(aw.shape, bf16),
            pltpu.VMEM(fw.shape, bf16),
            pltpu.VMEM((64, 256), bf16),
            pltpu.VMEM(pw.shape, bf16),
            pltpu.VMEM((768, 256), bf16),
            pltpu.VMEM((1024, 256), bf16),
            pltpu.VMEM((1024, 256), bf16),
            dma((11,)),
            dma((8,)), dma((8,)),
            dma((4,)), dma((4,)),
            dma((8,)), dma((8,)),
            dma((4,)), dma((4,)),
        ],
        compiler_params=pltpu.CompilerParams(
            collective_id=0, has_side_effects=True, vmem_limit_bytes=56 * 1024 * 1024
        ),
    )(
        lineup,
        pair.reshape(32, 128),
        keep.reshape(1, 32),
        mask.reshape(1, 32),
        chain.reshape(1, 32),
        intra,
        pbw.T,
        aw,
        fw,
        tw.T,
        pw,
    )
    return out, pair_out


def per_device(lineup, pair, *rest):
    axial, groups = lax.axis_size("axial"), lax.axis_size(("branch", "sub"))
    small = lineup.shape == (8, 4, 256) and pair.shape == (4, 8, 128)
    body = fused if small and axial == 8 and groups == 4 else shards
    return body(lineup, pair, *rest)


def solution(mesh):
    in_specs = (
        P(("branch", "sub"), "axial", None),
        P("axial", ("branch", "sub"), None),
        P(),
        P(),
        P(),
        P(),
        P(),
        P(),
        P(),
        P(),
        P(),
    )
    out_specs = (P(("branch", "sub"), "axial", None), P("axial", ("branch", "sub"), None))
    return jax.shard_map(
        per_device, mesh=mesh, in_specs=in_specs, out_specs=out_specs, check_vma=False
    )
```

```python
import jax
import jax.numpy as jnp
from jax import lax
from jax.experimental import pallas as pl
from jax.experimental.pallas import tpu as pltpu
from jax.sharding import PartitionSpec as P

HEAD_COUNT = 8
HEAD_SPAN = 32


def normalize_layer(values):
    values = values.astype(jnp.float32)
    average = jnp.mean(values, axis=-1, keepdims=True)
    centered = values - average
    variance = jnp.mean(centered * centered, axis=-1, keepdims=True)
    return centered * lax.rsqrt(variance + 1e-05)


def pair_bias(pair_features, chain_rows, chain_cols, intra_chain_bias, pair_bias_weight):
    standardized_embedding = normalize_layer(pair_features).astype(jnp.bfloat16)
    row_total, col_total, channels = standardized_embedding.shape
    biased = jnp.dot(
        standardized_embedding.reshape(row_total * col_total, channels),
        pair_bias_weight,
        preferred_element_type=jnp.float32,
    )
    biased = biased.reshape(row_total, col_total, -1)
    same_chain = (chain_rows[:, None] == chain_cols[None, :]).astype(jnp.float32)
    biased = biased + same_chain[:, :, None] * intra_chain_bias[None, None, :]
    return jnp.transpose(biased, (2, 0, 1)).astype(jnp.bfloat16)


def attend(
    row_values,
    normed_keys,
    normed_queries,
    bias,
    key_valid_mask,
    attention_weight,
    final_linear_matrix,
):
    seq_total, key_total, _ = normed_keys.shape
    query_total = normed_queries.shape[1]
    single_head_span = HEAD_COUNT * HEAD_SPAN
    key_values = jnp.einsum(
        "skc,cf->skf",
        normed_keys,
        attention_weight[:, single_head_span : 3 * single_head_span],
        preferred_element_type=jnp.float32,
    ).astype(jnp.bfloat16)
    w_query_gate = jnp.concatenate(
        (attention_weight[:, :single_head_span], attention_weight[:, 3 * single_head_span :]),
        axis=1,
    )
    fronts = jnp.einsum(
        "sqc,cf->sqf", normed_queries, w_query_gate, preferred_element_type=jnp.float32
    ).astype(jnp.bfloat16)
    key_heads = key_values.reshape(seq_total, key_total, 2, HEAD_COUNT, HEAD_SPAN).transpose(
        2, 3, 0, 1, 4
    )
    query_heads = fronts.reshape(seq_total, query_total, 2, HEAD_COUNT, HEAD_SPAN).transpose(
        2, 3, 0, 1, 4
    )
    scaling = 1.0 / HEAD_SPAN**0.5

    def one_head(operands):
        queries, key_side, val_side, bias_head = operands
        scores = jnp.einsum("sqd,skd->sqk", queries, key_side, preferred_element_type=jnp.float32)
        scores = (
            scores * scaling
            + bias_head.astype(jnp.float32)[None, :, :]
            + key_valid_mask[None, None, :]
        )
        maximum = jnp.max(scores, axis=-1, keepdims=True)
        expsum = jnp.exp(scores - maximum)
        weights = (expsum / jnp.sum(expsum, axis=-1, keepdims=True)).astype(jnp.bfloat16)
        return jnp.einsum("sqk,skd->sqd", weights, val_side, preferred_element_type=jnp.float32)

    attended = lax.map(one_head, (query_heads[0], key_heads[0], key_heads[1], bias))
    attended = attended.transpose(1, 2, 0, 3).reshape(seq_total, query_total, single_head_span)
    gate_side = (
        query_heads[1]
        .transpose(1, 2, 0, 3)
        .reshape(seq_total, query_total, single_head_span)
        .astype(jnp.float32)
    )
    gated_rows = (attended * jax.nn.sigmoid(gate_side)).astype(jnp.bfloat16)
    update = jnp.einsum(
        "sqf,fc->sqc", gated_rows, final_linear_matrix, preferred_element_type=jnp.float32
    )
    return (row_values.astype(jnp.float32) + update).astype(jnp.bfloat16)


def attend_whole(
    sequence_rows, combined_bias, key_valid_mask, attention_weight, final_linear_matrix
):
    standardized_embedding = normalize_layer(sequence_rows).astype(jnp.bfloat16)
    return attend(
        sequence_rows,
        standardized_embedding,
        standardized_embedding,
        combined_bias,
        key_valid_mask,
        attention_weight,
        final_linear_matrix,
    )


def outer_product_input(alignment_block, sequence_mask, position_mask, tensor_side_matrix):
    standardized_embedding = normalize_layer(alignment_block).astype(jnp.bfloat16)
    seq_total, res_total, feat_total = standardized_embedding.shape
    values = jnp.dot(
        standardized_embedding.reshape(seq_total * res_total, feat_total),
        tensor_side_matrix,
        preferred_element_type=jnp.float32,
    )
    values = values.reshape(seq_total, res_total, -1)
    weight = sequence_mask.astype(jnp.float32)[:, None] * position_mask.astype(jnp.float32)[None, :]
    return (values * weight[:, :, None]).astype(jnp.bfloat16)


def shards(
    lineup_embedding,
    pair_features,
    lineup_entry_keep,
    residue_mask,
    residue_chain_index,
    intra_chain_bias,
    pair_bias_weight,
    attention_weight,
    final_linear_matrix,
    tensor_side_matrix,
    outer_project_weight,
):
    group_index = lax.axis_index("branch") * lax.axis_size("sub") + lax.axis_index("sub")
    axial_index = lax.axis_index("axial")
    local_res = pair_features.shape[0]
    local_cols = pair_features.shape[1]
    sequence_group = lineup_embedding.shape[0]
    row_start = axial_index * local_res
    col_start = group_index * local_cols
    chain_rows = lax.dynamic_slice_in_dim(residue_chain_index, row_start, local_res)
    chain_cols = lax.dynamic_slice_in_dim(residue_chain_index, col_start, local_cols)
    local_bias = pair_bias(
        pair_features, chain_rows, chain_cols, intra_chain_bias, pair_bias_weight
    )
    key_valid_mask = (residue_mask.astype(jnp.float32) - 1.0) * 1000000000.0
    sequence_rows = lax.all_to_all(
        lineup_embedding, "axial", split_axis=0, concat_axis=1, tiled=True
    )
    partial_bias = lax.all_gather(local_bias, ("branch", "sub"), axis=2, tiled=True)
    combined_bias = lax.all_gather(partial_bias, "axial", axis=1, tiled=True)
    updated = attend_whole(
        sequence_rows, combined_bias, key_valid_mask, attention_weight, final_linear_matrix
    )
    pos_rows = lax.dynamic_slice_in_dim(residue_mask, row_start, local_res)
    pos_cols = lax.dynamic_slice_in_dim(residue_mask, col_start, local_cols)
    back_rows = lax.all_to_all(updated, "axial", split_axis=1, concat_axis=0, tiled=True)
    sequence_mask = lax.dynamic_slice_in_dim(
        lineup_entry_keep, group_index * sequence_group, sequence_group
    )
    factor_rows = outer_product_input(back_rows, sequence_mask, pos_rows, tensor_side_matrix)
    factor_width = factor_rows.shape[2] // 2
    left_flat = factor_rows[:, :, :factor_width].reshape(sequence_group, local_res * factor_width)
    right_all = lax.all_gather(factor_rows[:, :, factor_width:], "axial", axis=1, tiled=True)
    row_count = lax.axis_size(("branch", "sub")) * local_cols
    chosen = right_all
    chosen = chosen.reshape(sequence_group, row_count * factor_width)
    outer_sum = lax.dot_general(
        left_flat, chosen, (((0,), (0,)), ((), ())), preferred_element_type=jnp.float32
    )
    outer_sum = outer_sum.astype(jnp.bfloat16)
    arranged = outer_sum.reshape(local_res, factor_width, row_count, factor_width).transpose(
        2, 0, 1, 3
    )
    arranged = arranged.reshape(row_count * local_res, factor_width * factor_width)
    opm_total = lax.psum_scatter(
        jnp.dot(arranged, outer_project_weight, preferred_element_type=jnp.float32).reshape(
            row_count, local_res, -1
        ),
        ("branch", "sub"),
        scatter_dimension=0,
        tiled=True,
    )
    pair_sums = jnp.transpose(opm_total, (1, 0, 2))
    seq_count = jnp.sum(lineup_entry_keep.astype(jnp.float32))
    counted = (
        seq_count * pos_rows.astype(jnp.float32)[:, None] * pos_cols.astype(jnp.float32)[None, :]
    )
    pair_delta_update = (pair_sums / jnp.maximum(counted, 1.0)[:, :, None]).astype(jnp.bfloat16)
    return (back_rows, pair_delta_update)


def iota(shape, dim):
    return lax.broadcasted_iota(jnp.int32, shape, dim)


def mm(a, b):
    return jnp.dot(a, b, preferred_element_type=jnp.float32)


def mm_t(a, b):
    return lax.dot_general(a, b, (((1,), (1,)), ((), ())), preferred_element_type=jnp.float32)


def one_hot(cond):
    return jnp.where(cond, 1.0, 0.0).astype(jnp.bfloat16)


def pick_lanes(cond, row):
    return jnp.sum(jnp.where(cond, row, 0.0), axis=-1, keepdims=True)


def fused_kernel(
    own_hbm,
    pair_hbm,
    keep_hbm,
    mask_hbm,
    chain_hbm,
    intra_hbm,
    pbw_hbm,
    aw_hbm,
    fw_hbm,
    tw_hbm,
    pw_hbm,
    out_ref,
    pair_out_ref,
    own_ref,
    pair_ref,
    keep_ref,
    mask_ref,
    chain_ref,
    intra_ref,
    pbw_ref,
    msa,
    bias_part,
    bias_all,
    aligned,
    normed,
    partial,
    landed,
    aw,
    fw,
    tw,
    pw,
    aw_t,
    left_w,
    right_w,
    load_sem,
    msa_send,
    msa_recv,
    part_send,
    part_recv,
    all_send,
    all_recv,
    sum_send,
    sum_recv,
):
    f32, bf16 = jnp.float32, jnp.bfloat16
    axial = lax.axis_index("axial")
    n_axial = lax.axis_size("axial")
    n_sub = lax.axis_size("sub")
    group = lax.axis_index("branch") * n_sub + lax.axis_index("sub")
    n_group = lax.axis_size("branch") * n_sub
    axial_peers = [lax.rem(axial + d, n_axial) for d in range(n_axial)]
    group_peers = [lax.rem(group + d, n_group) for d in range(n_group)]

    def axial_id(d):
        return {"axial": axial_peers[d]}

    def group_id(d):
        return {"branch": group_peers[d] // n_sub, "sub": group_peers[d] % n_sub}

    loads = [
        pltpu.make_async_copy(src, dst, load_sem.at[n])
        for n, (src, dst) in enumerate(
            (
                (pair_hbm, pair_ref),
                (pbw_hbm, pbw_ref),
                (chain_hbm, chain_ref),
                (intra_hbm, intra_ref),
                (own_hbm, own_ref),
                (keep_hbm, keep_ref),
                (mask_hbm, mask_ref),
                (aw_hbm, aw),
                (tw_hbm, tw),
                (fw_hbm, fw),
                (pw_hbm, pw),
            )
        )
    ]
    barrier = pltpu.get_barrier_semaphore()
    for d in range(1, n_axial):
        pl.semaphore_signal(barrier, 1, device_id=axial_id(d), device_id_type=pl.DeviceIdType.MESH)
    for d in range(1, n_group):
        pl.semaphore_signal(barrier, 1, device_id=group_id(d), device_id_type=pl.DeviceIdType.MESH)
    for load in loads:
        load.start()
    for load in loads[:5]:
        load.wait()

    pair_rows = normalize_layer(pair_ref[...])
    padded = jnp.concatenate([pair_rows] * 4, axis=0).astype(bf16)
    local = mm_t(pbw_ref[...], padded)
    lane = iota((32, 128), 1)
    chain = jnp.broadcast_to(chain_ref[...].astype(f32), (8, 32)).astype(bf16)
    chain_i = mm(chain, one_hot(iota((32, 128), 0) == axial * 4 + ((lane >> 3) & 3)))
    chain_j = mm(chain, one_hot(iota((32, 128), 0) == group * 8 + (lane & 7)))
    head_row = iota((8, 128), 0)
    intra = jnp.zeros((8, 128), f32)
    for h in range(HEAD_COUNT):
        intra = jnp.where(head_row == h, intra_ref[h], intra)
    local = local + jnp.where(chain_i == chain_j, intra, 0.0)
    local = local.astype(bf16).astype(f32)
    local = jnp.where((iota((8, 128), 1) >> 5) == group, local, 0.0)
    bias_part[0] = local
    msa[:, axial] = own_ref[...].astype(f32).reshape(2, 16, 256).astype(bf16)

    pl.semaphore_wait(barrier, n_axial + n_group - 2)
    sends = []
    for d in range(1, n_group):
        copy = pltpu.make_async_remote_copy(
            bias_part.at[0], bias_part.at[d], part_send.at[d], part_recv.at[d],
            device_id=group_id(d), device_id_type=pl.DeviceIdType.MESH,
        )
        copy.start()
        sends.append(copy)
    part_copies = list(sends)
    msa_copies = []
    for d in range(1, n_axial):
        copy = pltpu.make_async_remote_copy(
            msa.at[:, axial], msa.at[:, axial], msa_send.at[d], msa_recv.at[d],
            device_id=axial_id(d), device_id_type=pl.DeviceIdType.MESH,
        )
        copy.start()
        sends.append(copy)
        msa_copies.append(copy)

    for load in loads[5:7]:
        load.wait()
    keep = keep_ref[...].astype(f32)
    mask = mask_ref[...].astype(f32)
    row = iota((256, 32), 0)
    lane32 = iota((256, 32), 1)
    row_mask = pick_lanes(lane32 == ((row >> 4) & 7) * 4 + (row & 3), mask)
    row_keep = pick_lanes(lane32 == group * 8 + (row >> 7) * 4 + ((row >> 2) & 3), keep)
    row_weight = row_keep * row_mask
    key_mask = (row_mask[:128] - 1.0) * 1000000000.0
    seq_count = jnp.sum(keep)
    for part in range(1, n_group):
        part_copies[part - 1].wait_recv()
    combined = bias_part[0]
    for part in range(1, n_group):
        combined = combined + bias_part[part]
    bias_all[axial] = combined
    all_copies = []
    for d in range(1, n_axial):
        copy = pltpu.make_async_remote_copy(
            bias_all.at[axial], bias_all.at[axial], all_send.at[d], all_recv.at[d],
            device_id=axial_id(d), device_id_type=pl.DeviceIdType.MESH,
        )
        copy.start()
        sends.append(copy)
        all_copies.append(copy)

    for load in loads[7:]:
        load.wait()
    for n, at in enumerate((0, 2, 3)):
        aw_t[n * 256 : (n + 1) * 256, :] = aw[:, at * 256 : (at + 1) * 256].T
    side = tw[...]
    rank, channel = iota((1024, 64), 0), iota((1024, 64), 1)
    left_w[...] = mm(one_hot(channel == (rank >> 5)), side).astype(bf16)
    right_w[...] = mm(one_hot(channel == 32 + (rank & 31)), side).astype(bf16)
    k_at, c_at = iota((128, 128), 0), iota((128, 128), 1)
    key_pick = one_hot((k_at >> 4) * 4 + (k_at & 3) == (c_at >> 5) * 8 + (c_at & 7))
    query_pick = ((c_at >> 3) & 3) == (k_at & 3)
    same_sequence = ((k_at >> 2) & 3) == ((c_at >> 2) & 3)

    for copy in msa_copies:
        copy.wait_recv()
    rows = msa[...].reshape(256, 256)
    rows_normed = normalize_layer(rows).astype(bf16)
    keys = mm(rows_normed, aw[:, 256:512]).astype(bf16)
    fronts = mm_t(aw_t[...], rows_normed).astype(bf16)
    gate_t = jax.nn.sigmoid(fronts[512:].astype(f32))

    for copy in all_copies:
        copy.wait_recv()
    scaling = 1.0 / HEAD_SPAN**0.5
    attended = [[], []]
    for h in range(HEAD_COUNT):
        spread = jnp.concatenate(
            [jnp.broadcast_to(bias_all[a, h : h + 1, :], (16, 128)) for a in range(8)], axis=0
        )
        spread = jnp.where(query_pick, spread, 0.0).astype(bf16)
        bias = jnp.where(same_sequence, mm_t(key_pick, spread), -1e30)
        lo, hi = h * HEAD_SPAN, (h + 1) * HEAD_SPAN
        for half in range(2):
            at = slice(half * 128, (half + 1) * 128)
            pieces = [fronts[lo:hi, at]]
            if lo:
                pieces.insert(0, jnp.zeros((lo, 128), bf16))
            if hi < 256:
                pieces.append(jnp.zeros((256 - hi, 128), bf16))
            scores = mm(keys[at], jnp.concatenate(pieces, axis=0)) * scaling + bias + key_mask
            raised = jnp.exp(scores - jnp.max(scores, axis=0, keepdims=True))
            weights = raised * (1.0 / jnp.sum(raised, axis=0, keepdims=True))
            attended[half].append(mm(fronts[256 + lo : 256 + hi, at], weights.astype(bf16)))
    attended_t = jnp.concatenate(
        [jnp.concatenate(attended[half], axis=0) for half in range(2)], axis=1
    )
    gated = (attended_t * gate_t).T.astype(bf16)
    updated = (rows.astype(f32) + mm(gated, fw[...])).astype(bf16)
    aligned[...] = updated.reshape(2, 8, 16, 256)
    out_ref[...] = aligned[:, axial].astype(f32).reshape(8, 4, 256).astype(bf16)
    side_in = (normalize_layer(updated) * row_weight).astype(bf16)
    normed[...] = side_in.reshape(2, 8, 16, 256)

    own_side = normed[:, axial].reshape(32, 256)
    r_at = iota((128, 32), 0)
    own_pick = one_hot(iota((128, 32), 1) == ((r_at >> 2) & 7) * 4 + (r_at >> 5))
    own_spread = mm(own_pick, own_side).astype(bf16)
    projected = jnp.zeros((256, 128), f32)
    for chunk in range(4):
        at = slice(chunk * 256, (chunk + 1) * 256)
        right = mm_t(side_in, right_w[at]).astype(bf16).astype(f32).reshape(2, 8, 2, 8, 256)
        left = mm_t(own_spread, left_w[at]).astype(bf16).astype(f32).reshape(4, 2, 2, 8, 256)
        outer = []
        for i in range(4):
            total = right[0, :, 0] * left[i, 0, 0][None]
            for half, two in ((0, 1), (1, 0), (1, 1)):
                total = total + right[half, :, two] * left[i, half, two][None]
            outer.append(total.reshape(64, 256))
        projected = projected + mm(jnp.concatenate(outer, axis=0).astype(bf16), pw[at, :])
    tiles = projected.reshape(4, 8, 8, 128)
    upper = iota((8, 128), 0) < 4
    for g in range(4):
        for i in range(4):
            one, two = tiles[i, 2 * g], tiles[i, 2 * g + 1]
            one = one + pltpu.roll(one, 4, 0)
            two = two + pltpu.roll(two, 4, 0)
            partial[g, i] = jnp.where(upper, one, two)
    sum_copies = []
    for d in range(1, n_group):
        copy = pltpu.make_async_remote_copy(
            partial.at[group_peers[d]], landed.at[d], sum_send.at[d], sum_recv.at[d],
            device_id=group_id(d), device_id_type=pl.DeviceIdType.MESH,
        )
        copy.start()
        sends.append(copy)
        sum_copies.append(copy)
    small_lane = iota((8, 32), 1)
    col_mask = pick_lanes(small_lane == group * 8 + iota((8, 32), 0), mask)
    counts = [
        jnp.maximum(seq_count * pick_lanes(small_lane == axial * 4 + i, mask) * col_mask, 1.0)
        for i in range(4)
    ]
    for copy in sum_copies:
        copy.wait_recv()
    total = partial[group] + landed[1] + landed[2] + landed[3]
    for i in range(4):
        pair_out_ref[i] = (total[i] / counts[i]).astype(bf16)
    for copy in sends:
        copy.wait_send()


def fused(lineup, pair, keep, mask, chain, intra, pbw, aw, fw, tw, pw):
    f32, bf16 = jnp.float32, jnp.bfloat16
    vmem = pl.BlockSpec(memory_space=pltpu.VMEM)
    hbm = pl.BlockSpec(memory_space=pltpu.HBM)
    dma = pltpu.SemaphoreType.DMA
    out, pair_out = pl.pallas_call(
        fused_kernel,
        out_shape=(
            jax.ShapeDtypeStruct(lineup.shape, bf16),
            jax.ShapeDtypeStruct((4, 8, 128), bf16),
        ),
        in_specs=[hbm] * 11,
        out_specs=(vmem, vmem),
        scratch_shapes=[
            pltpu.VMEM(lineup.shape, bf16),
            pltpu.VMEM((32, 128), bf16),
            pltpu.VMEM((1, 32), jnp.int32),
            pltpu.VMEM((1, 32), jnp.int32),
            pltpu.VMEM((1, 32), jnp.int32),
            pltpu.SMEM((HEAD_COUNT,), f32),
            pltpu.VMEM((HEAD_COUNT, 128), bf16),
            pltpu.VMEM((2, 8, 16, 256), bf16),
            pltpu.VMEM((4, 8, 128), f32),
            pltpu.VMEM((8, 8, 128), f32),
            pltpu.VMEM((2, 8, 16, 256), bf16),
            pltpu.VMEM((2, 8, 16, 256), bf16),
            pltpu.VMEM((4, 4, 8, 128), f32),
            pltpu.VMEM((4, 4, 8, 128), f32),
            pltpu.VMEM(aw.shape, bf16),
            pltpu.VMEM(fw.shape, bf16),
            pltpu.VMEM((64, 256), bf16),
            pltpu.VMEM(pw.shape, bf16),
            pltpu.VMEM((768, 256), bf16),
            pltpu.VMEM((1024, 256), bf16),
            pltpu.VMEM((1024, 256), bf16),
            dma((11,)),
            dma((8,)), dma((8,)),
            dma((4,)), dma((4,)),
            dma((8,)), dma((8,)),
            dma((4,)), dma((4,)),
        ],
        compiler_params=pltpu.CompilerParams(
            collective_id=0, has_side_effects=True, vmem_limit_bytes=56 * 1024 * 1024
        ),
    )(
        lineup,
        pair.reshape(32, 128),
        keep.reshape(1, 32),
        mask.reshape(1, 32),
        chain.reshape(1, 32),
        intra,
        pbw.T,
        aw,
        fw,
        tw.T,
        pw,
    )
    return out, pair_out


def per_device(lineup, pair, *rest):
    axial, groups = lax.axis_size("axial"), lax.axis_size(("branch", "sub"))
    small = lineup.shape == (8, 4, 256) and pair.shape == (4, 8, 128)
    body = fused if small and axial == 8 and groups == 4 else shards
    return body(lineup, pair, *rest)


def solution(mesh):
    in_specs = (
        P(("branch", "sub"), "axial", None),
        P("axial", ("branch", "sub"), None),
        P(),
        P(),
        P(),
        P(),
        P(),
        P(),
        P(),
        P(),
        P(),
    )
    out_specs = (P(("branch", "sub"), "axial", None), P("axial", ("branch", "sub"), None))
    return jax.shard_map(
        per_device, mesh=mesh, in_specs=in_specs, out_specs=out_specs, check_vma=False
    )
```
